32 devices in a mesh: fsdp: 16 (over z, y, x), tp: 2 (over core).
Axes of the slice: x: 2, y: 2, z: 4, core: 2. Of those that a mesh axis runs over, the one named last changes fastest.
Arguments:
- tokens: bfloat16 [8192, 768], P(('fsdp', 'tp')), may hold values from -6 to 6
- cotangent: bfloat16 [8192, 768], P(('fsdp', 'tp')), may hold values from -6 to 6
- gain_attn: bfloat16 [768], replicated, may hold values from 0.25 to 1.75
- gain_moe: bfloat16 [768], replicated, may hold values from 0.25 to 1.75
- w_query: bfloat16 [768, 768], P('fsdp', 'tp'), may hold values from -0.21875 to 0.21875
- w_key: bfloat16 [768, 768], P('fsdp', 'tp'), may hold values from -0.21875 to 0.21875
- w_value: bfloat16 [768, 768], P('fsdp', 'tp'), may hold values from -0.21875 to 0.21875
- w_output: bfloat16 [768, 768], P('tp', 'fsdp'), may hold values from -0.875 to 0.875
- bias_table: bfloat16 [32, 12], P(None, 'tp'), may hold values from -4 to 4
- router: bfloat16 [768, 4], replicated, may hold values from -0.15625 to 0.15625
- w_in: bfloat16 [4, 768, 3072], P(None, 'fsdp', 'tp'), may hold values from -0.21875 to 0.21875
- w_out: bfloat16 [4, 3072, 768], P(None, 'tp', 'fsdp'), may hold values from -0.4375 to 0.4375
- lengths: int32 [16, 4], P('fsdp'), may hold values from 1 to 256, as said below
- routes: int32 [8192], P('fsdp'), may hold values from 0 to 3
- slots: int32 [8192], P('fsdp'), may hold values from -1 to 191, as said below
- buckets: int32 [511], replicated, may hold values from 0 to 31
Outputs:
- output: bfloat16 [8192, 768], P(('fsdp', 'tp'))
- grad_tokens: float32 [8192, 768], P(('fsdp', 'tp'))
- grad_gain_attn: float32 [768], replicated
- grad_gain_moe: float32 [768], replicated
- grad_w_query: float32 [768, 768], P('fsdp', 'tp')
- grad_w_key: float32 [768, 768], P('fsdp', 'tp')
- grad_w_value: float32 [768, 768], P('fsdp', 'tp')
- grad_w_output: float32 [768, 768], P('tp', 'fsdp')
- grad_bias_table: float32 [32, 12], P(None, 'tp')
- grad_router: float32 [768, 4], replicated
- grad_w_in: float32 [4, 768, 3072], P(None, 'fsdp', 'tp')
- grad_w_out: float32 [4, 3072, 768], P(None, 'tp', 'fsdp')
The draws below stay inside these ranges and needn't reach their ends.
Inputs may be any that keep to these rules, and one draw needn't show every extreme that they name: Each group holds 4 sequences whose lengths sum to 512; the second is the longest, of exactly 256 tokens. A token's slot is the number of earlier tokens of its group with the same route, or -1 where that number is 192 or more; in every group some expert fills all 192 slots.
All inputs are finite; a program needn't handle non-finite values.
Results may differ from the reference program's by a relative error of at most 0.013.
Values may be sent and summed in bfloat16 or wider, within the bound.
A program may use at most 256 MiB of HBM per device.

```python
import math
import jax
import jax.numpy as jnp
from jax import lax

D = 768
HEADS = 12
HD = 64
FF = 3072
NB = 32
EXPERTS = 4
TOK_DEV = 256
ROWS_GRP = 512
MAXLEN = 256
CAP = 192
TOKENS = 8192
N_FSDP = 16
N_TP = 2


def route_pair(key):
    group_count = TOKENS // ROWS_GRP
    hot_expert = jax.random.randint(jax.random.fold_in(key, 11), (group_count, 1), 0, EXPERTS)
    other_expert = jax.random.randint(jax.random.fold_in(key, 12), (group_count, ROWS_GRP), 0, EXPERTS)
    phase = jax.random.randint(jax.random.fold_in(key, 13), (group_count, 1), 0, 2)
    places = jnp.arange(ROWS_GRP, dtype=jnp.int32)[None, :]
    route_ids = jnp.where((places + phase) % 2 == 0, hot_expert, other_expert).astype(jnp.int32)
    hot_table = (route_ids[:, :, None] == jnp.arange(EXPERTS, dtype=jnp.int32)[None, None, :]).astype(jnp.int32)
    ranks = jnp.sum((jnp.cumsum(hot_table, axis=1) - 1) * hot_table, axis=2)
    slot_ids = jnp.where(ranks < CAP, ranks, -1).astype(jnp.int32)
    return (route_ids.reshape(-1), slot_ids.reshape(-1))


def draw_routes(key, part):
    return route_pair(key)[0]


def draw_slots(key, part):
    return route_pair(key)[1]


def draw_lengths(key, part):
    key = jax.random.fold_in(key, 5)
    group_count = TOKENS // ROWS_GRP
    first_len = jax.random.randint(jax.random.fold_in(key, 1), (group_count,), 1, MAXLEN - 1)
    remainder = ROWS_GRP - MAXLEN - first_len
    third_len = jax.random.randint(jax.random.fold_in(key, 2), (group_count,), 1, remainder)
    fourth_len = remainder - third_len
    longest = jnp.full((group_count,), MAXLEN, jnp.int32)
    return jnp.stack([first_len, longest, third_len, fourth_len], axis=1).astype(jnp.int32)


def place_ends(entries, stream_key, low, largest):
    longest = entries.shape.index(max(entries.shape))
    spots = []
    for shift in (0, 1):
        where = [jax.random.randint(jax.random.fold_in(stream_key, axis), (), 0, length) for axis, length in enumerate(entries.shape)]
        where[longest] = (where[longest] + shift) % entries.shape[longest]
        spots.append(tuple(where))
    return entries.at[spots[0]].set(low).at[spots[1]].set(largest)


def steps_of(key, dims, shards, least, top_value):
    level = 1.0
    for position, parts in shards:
        steps = jax.random.uniform(jax.random.fold_in(jax.random.fold_in(key, 6), position), (parts,), jnp.float32, least / len(shards), top_value / len(shards))
        level = level * jnp.repeat(jnp.exp(steps), dims[position] // parts).reshape((-1,) + (1,) * (len(dims) - 1 - position))
    return level


def bell_draw(stream_key, extent, scale, limit, split=(), kind=jnp.bfloat16):
    drawn = jax.random.normal(stream_key, extent, jnp.float32) * scale
    if len(split) > 0:
        drawn = steps_of(stream_key, extent, split, -0.22, 0.18) * drawn
    return jnp.clip(drawn, min=-limit, max=limit).astype(kind)


def setup_inputs(seed: int = 0) -> dict:
    key_of = jax.random.split(jax.random.key(seed), 17)
    tokens = bell_draw(key_of[0], (TOKENS, D), 1.0, 6.0, ((0, 32),))
    cotangent = bell_draw(key_of[1], (TOKENS, D), 1.0, 6.0, ((0, 32),))
    gain_attn = jnp.clip(1.0 + 0.15 * jax.random.normal(key_of[2], (D,), jnp.float32), 0.25, 1.75).astype(jnp.bfloat16)
    gain_moe = jnp.clip(1.0 + 0.15 * jax.random.normal(key_of[3], (D,), jnp.float32), 0.25, 1.75).astype(jnp.bfloat16)
    w_query = bell_draw(key_of[4], (D, D), D ** -0.5, 0.21875, ((0, 16), (1, 2)))
    w_key = bell_draw(key_of[5], (D, D), D ** -0.5, 0.21875, ((0, 16), (1, 2)))
    w_value = bell_draw(key_of[6], (D, D), D ** -0.5, 0.21875, ((0, 16), (1, 2)))
    w_output = bell_draw(key_of[7], (D, D), (D // 16) ** -0.5, 0.875, ((0, 2), (1, 16)))
    bias_table = bell_draw(key_of[8], (NB, HEADS), 1.0, 4.0, ((1, 2),))
    router = bell_draw(key_of[9], (D, EXPERTS), (2 * D) ** -0.5, 0.15625)
    w_in = bell_draw(key_of[10], (EXPERTS, D, FF), D ** -0.5, 0.21875, ((1, 16), (2, 2)))
    w_out = bell_draw(key_of[11], (EXPERTS, FF, D), (FF // 16) ** -0.5, 0.4375, ((1, 2), (2, 16)))
    lengths = draw_lengths(jax.random.fold_in(key_of[16], 71), 0)
    routes = draw_routes(jax.random.fold_in(key_of[16], 71), 0)
    slots = draw_slots(jax.random.fold_in(key_of[16], 71), 0)
    buckets = place_ends(jax.random.randint(key_of[15], (2 * MAXLEN - 1,), 0, NB), jax.random.fold_in(key_of[15], 1), 0, NB - 1).astype(jnp.int32)
    return {"tokens": tokens, "cotangent": cotangent, "gain_attn": gain_attn, "gain_moe": gain_moe, "w_query": w_query, "w_key": w_key, "w_value": w_value, "w_output": w_output, "bias_table": bias_table, "router": router, "w_in": w_in, "w_out": w_out, "lengths": lengths, "routes": routes, "slots": slots, "buckets": buckets}


@jax.custom_vjp
def low(v):
    return lax.optimization_barrier(v.astype(jnp.bfloat16)).astype(jnp.float32)

@jax.custom_vjp
def low_back(v):
    return v

def low_keep(v):
    return (low(v), None)

def low_pass(kept, grad):
    return (grad,)

def back_keep(v):
    return (v, None)

def back_low(kept, grad):
    return (low(grad),)
low.defvjp(low_keep, low_pass)
low_back.defvjp(back_keep, back_low)
EPSILON = 1e-06
MASKED = -1e+30
HIGHEST = lax.Precision.HIGHEST

def matmul_high(left, right):
    return jnp.dot(left, right, precision=HIGHEST)

def rms_normed(values, gain_vec):
    normed = values * lax.rsqrt(lax.optimization_barrier(jnp.mean(values * values, axis=-1, keepdims=True)) + EPSILON)
    return low(normed * gain_vec)

def reference(tokens, cotangent, gain_attn, gain_moe, w_query, w_key, w_value, w_output, bias_table, router, w_in, w_out, lengths, routes, slots, buckets):
    group_rows = TOK_DEV * N_TP
    group_count = N_FSDP
    block_rows = min(512, group_rows)
    slot_count = EXPERTS * CAP
    score_scale = 1.0 / math.sqrt(HD)
    positions = jnp.arange(group_rows, dtype=jnp.int32)
    expert_ids = jnp.arange(EXPERTS, dtype=jnp.int32)

    def layer_group(weights, values, seq_lens, route_ids, slot_ids):
        gain_one, gain_two, query_w, key_w, value_w, output_w, table_w, router_w, inner_w, outer_w = weights
        normed_one = rms_normed(values, gain_one)
        queries = low(low_back(matmul_high(normed_one, query_w))).reshape(group_rows, HEADS, HD)
        keys_all = low(low_back(matmul_high(normed_one, key_w))).reshape(group_rows, HEADS, HD)
        values_all = low(low_back(matmul_high(normed_one, value_w))).reshape(group_rows, HEADS, HD)
        bounds = jnp.cumsum(seq_lens)
        segment = lax.optimization_barrier(jnp.sum((positions[:, None] >= bounds[None, :]).astype(jnp.int32), axis=1))
        relative = table_w[buckets]

        def attend(first_row):
            query_blk = lax.dynamic_slice_in_dim(queries, first_row, block_rows, 0)
            query_pos = first_row + jnp.arange(block_rows, dtype=jnp.int32)
            offsets = jnp.clip(positions[None, :] - query_pos[:, None] + MAXLEN - 1, 0, 2 * MAXLEN - 2)
            bias_blk = jnp.transpose(relative[offsets], (2, 0, 1))
            raw_scores = low_back(jnp.einsum('qhd,khd->hqk', query_blk, keys_all, precision=HIGHEST) * score_scale + bias_blk)
            same_seq = lax.dynamic_slice_in_dim(segment, first_row, block_rows, 0)[:, None] == segment[None, :]
            masked = jnp.where(same_seq[None], raw_scores, MASKED)
            weights_p = low(jax.nn.softmax(masked, axis=-1))
            return jnp.einsum('hqk,khd->qhd', weights_p, values_all, precision=HIGHEST)
        block_starts = jnp.arange(group_rows // block_rows, dtype=jnp.int32) * block_rows
        mixed_out = lax.map(jax.checkpoint(attend), block_starts).reshape(group_rows, HEADS * HD)
        mixed_out = low(low_back(mixed_out))
        hidden = values + low_back(matmul_high(mixed_out, output_w))
        normed_two = rms_normed(hidden, gain_two)
        chances = jax.nn.softmax(low_back(matmul_high(normed_two, router_w)), axis=-1)
        onehot = (route_ids[:, None] == expert_ids[None, :]).astype(values.dtype)
        gate_val = lax.optimization_barrier(jnp.sum(chances * onehot, axis=-1))
        kept_mask = slot_ids >= 0
        places = route_ids * CAP + slot_ids
        target = jnp.where(kept_mask, places, slot_count)
        slot_owner = jnp.zeros((slot_count + 1,), jnp.int32).at[target].set(positions)[:slot_count]
        filled = jnp.zeros((slot_count + 1,), values.dtype).at[target].set(1.0)[:slot_count]
        buffer = (normed_two[slot_owner] * filled[:, None]).reshape(EXPERTS, CAP, D)
        pre_act = low_back(jnp.einsum('ecd,edf->ecf', buffer, inner_w, precision=HIGHEST))
        activated = low(jax.nn.gelu(pre_act))
        expert_rows = jnp.einsum('ecf,efd->ecd', activated, outer_w, precision=HIGHEST).reshape(slot_count, D)
        slot_pick = jnp.where(kept_mask, places, 0)
        expert_val = low_back(expert_rows[slot_pick] * kept_mask.astype(values.dtype)[:, None])
        return hidden + gate_val[:, None] * expert_val

    def forward(inputs, *weights):

        def group_step(carry_in, pieces):
            return (carry_in, layer_group(weights, *pieces))
        stacked = (inputs.reshape(group_count, group_rows, D), lengths, routes.reshape(group_count, group_rows), slots.reshape(group_count, group_rows))
        _, results = lax.scan(jax.checkpoint(group_step), None, stacked)
        return results.reshape(group_count * group_rows, D)
    arguments = tuple((item.astype(jnp.float32) for item in (tokens, gain_attn, gain_moe, w_query, w_key, w_value, w_output, bias_table, router, w_in, w_out)))
    results, pullback = jax.vjp(forward, *arguments)
    gradients = pullback(cotangent.astype(jnp.float32))
    return (results.astype(jnp.bfloat16), gradients[0], gradients[1], gradients[2], gradients[3], gradients[4], gradients[5], gradients[6], gradients[7], gradients[8], gradients[9], gradients[10])
```

```python
import functools
import math

import jax
import jax.numpy as jnp
from jax import lax
from jax.experimental import pallas as pl
from jax.experimental.pallas import tpu as pltpu
from jax.sharding import PartitionSpec as P

HD = 64
CAP = 192
EPSILON = 1e-06
MASKED = -1e30
HIGHEST = lax.Precision.HIGHEST
F32 = jnp.float32
BF16 = jnp.bfloat16
NT = (((1,), (1,)), ((), ()))
TN = (((0,), (0,)), ((), ()))


def rms_stats(values):
    inverse = lax.rsqrt(jnp.mean(values * values, axis=-1, keepdims=True) + EPSILON)
    return (values * inverse, inverse)


def rms_back(grad_hat, normed, inverse):
    return inverse * (grad_hat - normed * jnp.mean(grad_hat * normed, axis=-1, keepdims=True))


def tp_swap(values):
    return lax.ppermute(values, "tp", [(0, 1), (1, 0)])


def tp_gather(values):
    other = tp_swap(values)
    first = lax.axis_index("tp") == 0
    low = jnp.where(first, values, other)
    high = jnp.where(first, other, values)
    return jnp.concatenate([low, high], axis=0)


def tp_scatter(values):
    half = values.shape[0] // 2
    me = lax.axis_index("tp")
    away = lax.dynamic_slice_in_dim(values, (1 - me) * half, half, 0)
    keep = lax.dynamic_slice_in_dim(values, me * half, half, 0)
    return keep + tp_swap(away)


def fsdp_gather(shard):
    return lax.all_gather(shard, "fsdp", axis=0, tiled=False)


def add_low(left, right):
    return (left.astype(F32) + right.astype(F32)).astype(BF16)


def scatter_grid(blocks):
    index = lax.axis_index("fsdp")
    z_at, y_at, x_at = index // 4, (index // 2) % 2, index % 2
    grid = blocks.reshape((4, 2, 2) + blocks.shape[1:])
    half = blocks.shape[1] // 2

    def flip(values, bit):
        return lax.ppermute(values, "fsdp", [(i, i ^ bit) for i in range(16)])

    def fold(part, place, axis, bit):
        away = lax.dynamic_index_in_dim(part, 1 - place, axis, False)
        keep = lax.dynamic_index_in_dim(part, place, axis, False)
        return add_low(keep, flip(away, bit))

    first = fold(fold(grid[:, :, :, :half], x_at, 2, 1), y_at, 1, 2)
    second = fold(fold(grid[:, :, :, half:], y_at, 1, 2), x_at, 1, 1)
    column = jnp.concatenate([first, second], axis=1)

    def pick(target):
        return lax.dynamic_index_in_dim(column, jnp.clip(target, 0, 3), 0, False)

    rising = falling = None
    for offset in (3, 2, 1):
        up, down = pick(z_at + offset), pick(z_at - offset)
        if rising is not None:
            up, down = add_low(up, rising), add_low(down, falling)
        rising = lax.ppermute(
            up, "fsdp", [(i, i + 4) for i in range(12) if i // 4 + offset <= 3]
        )
        falling = lax.ppermute(
            down, "fsdp", [(i, i - 4) for i in range(4, 16) if i // 4 - offset >= 0]
        )
    return pick(z_at).astype(F32) + rising.astype(F32) + falling.astype(F32)


def fsdp_scatter(blocks):
    if USE_GRID and blocks.shape[0] == 16:
        return scatter_grid(blocks.astype(BF16))
    low = blocks.astype(BF16)
    flat = low.reshape((-1, low.shape[-1]))
    return lax.psum_scatter(flat, "fsdp", scatter_dimension=0, tiled=True).astype(F32).reshape(
        blocks.shape[1:]
    )


def head_weights(query, key, window, same, rows):
    scale = 1.0 / math.sqrt(HD)
    skew = pltpu.roll(
        jnp.broadcast_to(window, (rows, rows)), 0, 1, stride=1, stride_axis=0
    )
    scores = lax.dot_general(query, key, NT, preferred_element_type=F32) * scale + skew
    scores = jnp.where(same, scores, MASKED)
    raised = jnp.exp(scores - jnp.max(scores, axis=-1, keepdims=True))
    return raised / jnp.sum(raised, axis=-1, keepdims=True)


def attend_kernel(q_ref, k_ref, v_ref, win_ref, col_ref, row_ref, o_ref):
    rows = q_ref.shape[0]
    same = col_ref[...] == row_ref[...]
    mixed = []
    for head in range(2):
        part = slice(head * HD, (head + 1) * HD)
        weights = head_weights(
            q_ref[:, part], k_ref[:, part], win_ref[0, head : head + 1, :], same, rows
        )
        mixed.append(
            jnp.dot(weights.astype(BF16), v_ref[:, part], preferred_element_type=F32)
        )
    o_ref[...] = jnp.concatenate(mixed, axis=1).astype(BF16)


def attend_back_kernel(
    q_ref, k_ref, v_ref, do_ref, win_ref, col_ref, row_ref, dq_ref, dk_ref, dv_ref, sums_ref
):
    rows = q_ref.shape[0]
    scale = 1.0 / math.sqrt(HD)
    same = col_ref[...] == row_ref[...]
    all_dq, all_dk, all_dv, all_sums = [], [], [], []
    for head in range(2):
        part = slice(head * HD, (head + 1) * HD)
        query, key, value, grad = q_ref[:, part], k_ref[:, part], v_ref[:, part], do_ref[:, part]
        weights = head_weights(query, key, win_ref[0, head : head + 1, :], same, rows)
        low = weights.astype(BF16)
        grad_weights = lax.dot_general(grad, value, NT, preferred_element_type=F32)
        inner = jnp.sum(weights * grad_weights, axis=-1, keepdims=True)
        grad_scores = (weights * (grad_weights - inner)).astype(BF16)
        all_dq.append(jnp.dot(grad_scores, key, preferred_element_type=F32) * scale)
        all_dk.append(
            lax.dot_general(grad_scores, query, TN, preferred_element_type=F32) * scale
        )
        all_dv.append(lax.dot_general(low, grad, TN, preferred_element_type=F32))
        fold = grad_scores.astype(F32)
        count = rows
        while count > 8:
            count //= 2
            fold = fold[:count] + pltpu.roll(fold[count:], rows - count, 1)
        total = fold[0:1]
        for line in range(1, 8):
            total = total + pltpu.roll(fold, rows - line, 1)[line : line + 1]
        all_sums.append(total)
    dq_ref[...] = jnp.concatenate(all_dq, axis=1).astype(BF16)
    dk_ref[...] = jnp.concatenate(all_dk, axis=1).astype(BF16)
    dv_ref[...] = jnp.concatenate(all_dv, axis=1).astype(BF16)
    sums_ref[0] = jnp.concatenate(all_sums, axis=0)


def attend_call(kernel, wide_out, sums_out, wide_in, window, seg_col, seg_row):
    rows, width = wide_in[0].shape
    steps = width // (2 * HD)
    wide = pl.BlockSpec((rows, 2 * HD), lambda i: (0, i))
    lines = pl.BlockSpec((1, 2, rows), lambda i: (i, 0, 0))
    flops = 2 * 2 * rows * rows * width * (2 if wide_out == 1 else 5)
    return pl.pallas_call(
        kernel,
        grid=(steps,),
        in_specs=[wide] * len(wide_in)
        + [
            lines,
            pl.BlockSpec((rows, 1), lambda i: (0, 0)),
            pl.BlockSpec((1, rows), lambda i: (0, 0)),
        ],
        out_specs=[wide] * wide_out + [lines] * sums_out,
        out_shape=[jax.ShapeDtypeStruct((rows, width), BF16)] * wide_out
        + [jax.ShapeDtypeStruct((steps, 2, rows), F32)] * sums_out,
        cost_estimate=pl.CostEstimate(
            flops=flops, bytes_accessed=2 * rows * width * 8, transcendentals=rows * rows * 6
        ),
        compiler_params=pltpu.CompilerParams(vmem_limit_bytes=48 * 1024 * 1024),
    )(*wide_in, window, seg_col, seg_row)


def on_device(
    tokens,
    cotangent,
    gain_attn,
    gain_moe,
    w_query,
    w_key,
    w_value,
    w_output,
    bias_table,
    router,
    w_in,
    w_out,
    lengths,
    routes,
    slots,
    buckets,
):
    row_count, model_width = tokens.shape
    group_rows = routes.shape[0]
    bucket_count, head_count = bias_table.shape
    expert_count = router.shape[1]
    slot_count = expert_count * CAP
    hidden_width = w_in.shape[2]
    head_width = w_query.shape[1]
    shard_rows = w_query.shape[0]
    n_fsdp = lax.axis_size("fsdp")
    span_len = buckets.shape[0]
    max_len = (span_len + 1) // 2
    tp_index = lax.axis_index("tp")
    positions = jnp.arange(group_rows, dtype=jnp.int32)
    expert_ids = jnp.arange(expert_count, dtype=jnp.int32)

    attn_shard = jnp.stack([w_query, w_key, w_value, w_output.T])
    attn_all = fsdp_gather(attn_shard)
    inner_all = fsdp_gather(w_in)
    outer_all = fsdp_gather(jnp.transpose(w_out, (0, 2, 1)))
    attn_full = jnp.transpose(attn_all, (1, 0, 2, 3)).reshape(4, model_width, head_width)
    inner_full = jnp.transpose(inner_all, (1, 0, 2, 3)).reshape(
        expert_count, model_width, hidden_width
    )
    outer_full = jnp.transpose(outer_all, (1, 0, 2, 3)).reshape(
        expert_count, model_width, hidden_width
    )

    inputs = tokens.astype(F32)
    gain_one = gain_attn.astype(F32)
    gain_two = gain_moe.astype(F32)
    normed_one, inverse_one = rms_stats(inputs)
    scaled_one = (normed_one * gain_one).astype(BF16)
    rows_one = tp_gather(scaled_one)

    bounds = jnp.cumsum(lengths[0])
    segment = jnp.sum((positions[:, None] >= bounds[None, :]).astype(jnp.int32), axis=1)
    seg_col, seg_row = segment[:, None], segment[None, :]
    bucket_ids = jnp.arange(bucket_count, dtype=jnp.int32)
    window_buckets = jnp.concatenate(
        [
            buckets[max_len - 1 :],
            jnp.full((group_rows - span_len,), -1, jnp.int32),
            buckets[: max_len - 1],
        ]
    )
    window_hot = (window_buckets[:, None] == bucket_ids[None, :]).astype(F32)
    window = jnp.dot(window_hot, bias_table.astype(F32), precision=HIGHEST).T.reshape(
        head_count // 2, 2, group_rows
    )

    queries, keys_all, values_all = (
        jnp.dot(rows_one, attn_full[i], preferred_element_type=F32).astype(BF16) for i in range(3)
    )
    (mixed_out,) = attend_call(
        attend_kernel, 1, 0, (queries, keys_all, values_all), window, seg_col, seg_row
    )
    attn_part = lax.dot_general(mixed_out, attn_full[3], NT, preferred_element_type=F32)
    hidden = inputs + tp_scatter(attn_part)
    normed_two, inverse_two = rms_stats(hidden)
    scaled_two = (normed_two * gain_two).astype(BF16)
    rows_two = tp_gather(scaled_two)

    own_routes = lax.dynamic_slice_in_dim(routes, tp_index * row_count, row_count, 0)
    chances = jax.nn.softmax(jnp.dot(scaled_two, router, preferred_element_type=F32), axis=-1)
    own_hot = (own_routes[:, None] == expert_ids[None, :]).astype(F32)
    gate_val = jnp.sum(chances * own_hot, axis=-1, keepdims=True)

    kept_mask = slots >= 0
    places = jnp.where(kept_mask, routes * CAP + slots, -1)
    slot_ids = jnp.arange(slot_count, dtype=jnp.int32)
    dispatch = (slot_ids[:, None] == places[None, :]).astype(BF16)
    collect = (places[:, None] == slot_ids[None, :]).astype(BF16)

    def to_slots(rows):
        return (
            jnp.dot(dispatch, rows, preferred_element_type=F32)
            .astype(BF16)
            .reshape(expert_count, CAP, model_width)
        )

    def to_tokens(rows):
        high = rows.astype(BF16)
        low = (rows - high.astype(F32)).astype(BF16)
        return jnp.dot(collect, high, preferred_element_type=F32) + jnp.dot(
            collect, low, preferred_element_type=F32
        )

    buffer = to_slots(rows_two)
    pre_act = jnp.einsum("ecd,edf->ecf", buffer, inner_full, preferred_element_type=F32)
    activated = jax.nn.gelu(pre_act).astype(BF16)
    expert_rows = jnp.einsum(
        "ecf,edf->ecd", activated, outer_full, preferred_element_type=F32
    ).reshape(slot_count, model_width)
    expert_val = tp_scatter(to_tokens(expert_rows))
    result = hidden + gate_val * expert_val

    grad_out = cotangent.astype(F32)
    grad_gate = jnp.sum(grad_out * expert_val, axis=-1, keepdims=True)
    grad_expert = (gate_val * grad_out).astype(BF16)
    grad_slots = to_slots(tp_gather(grad_expert))

    def blocked(grads, parts):
        return jnp.transpose(
            grads.astype(BF16).reshape(parts, n_fsdp, shard_rows, grads.shape[-1]), (1, 0, 2, 3)
        )

    grad_outer = jnp.einsum("ecd,ecf->edf", grad_slots, activated, preferred_element_type=F32)
    outer_sum = fsdp_scatter(blocked(grad_outer, expert_count))
    grad_act = jnp.einsum("ecd,edf->ecf", grad_slots, outer_full, preferred_element_type=F32)
    grad_pre = jax.vjp(jax.nn.gelu, pre_act)[1](grad_act)[0].astype(BF16)
    grad_inner = jnp.einsum("ecd,ecf->edf", buffer, grad_pre, preferred_element_type=F32)
    inner_sum = fsdp_scatter(blocked(grad_inner, expert_count))
    grad_buffer = jnp.einsum(
        "ecf,edf->ecd", grad_pre, inner_full, preferred_element_type=F32
    ).reshape(slot_count, model_width)
    grad_logits = (grad_gate * gate_val * (own_hot - chances)).astype(BF16)
    grad_router = jnp.einsum("td,te->de", scaled_two, grad_logits, preferred_element_type=F32)
    grad_scaled_two = tp_scatter(to_tokens(grad_buffer)) + jnp.einsum(
        "te,de->td", grad_logits, router, preferred_element_type=F32
    )
    grad_gain_two = jnp.sum(grad_scaled_two * normed_two, axis=0)
    grad_hidden = grad_out + rms_back(grad_scaled_two * gain_two, normed_two, inverse_two)
    grad_attn = tp_gather(grad_hidden.astype(BF16))
    grad_mixed = jnp.dot(grad_attn, attn_full[3], preferred_element_type=F32).astype(BF16)
    grad_queries, grad_keys, grad_values, window_sums = attend_call(
        attend_back_kernel,
        3,
        1,
        (queries, keys_all, values_all, grad_mixed),
        window,
        seg_col,
        seg_row,
    )
    attn_grads = jnp.stack(
        [
            lax.dot_general(left, right, TN, preferred_element_type=F32)
            for left, right in (
                (rows_one, grad_queries),
                (rows_one, grad_keys),
                (rows_one, grad_values),
                (grad_attn, mixed_out),
            )
        ]
    )
    attn_sum = fsdp_scatter(blocked(attn_grads, 4))
    grad_one_part = sum(
        lax.dot_general(grads, attn_full[i], NT, preferred_element_type=F32)
        for i, grads in enumerate((grad_queries, grad_keys, grad_values))
    )
    grad_scaled_one = tp_scatter(grad_one_part)
    grad_gain_one = jnp.sum(grad_scaled_one * normed_one, axis=0)
    grad_inputs = grad_hidden + rms_back(grad_scaled_one * gain_one, normed_one, inverse_one)

    grad_table_here = jnp.dot(
        window_sums.reshape(head_count, group_rows), window_hot, precision=HIGHEST
    )
    table_full = lax.dynamic_update_slice_in_dim(
        jnp.zeros((head_count * lax.axis_size("tp"), bucket_count), F32),
        grad_table_here,
        tp_index * head_count,
        0,
    )
    pieces = [grad_gain_one, grad_gain_two, grad_router.T.reshape(-1), table_full.reshape(-1)]
    small = lax.psum(jnp.concatenate(pieces), ("fsdp", "tp"))
    split = [0]
    for piece in pieces:
        split.append(split[-1] + piece.shape[0])
    total_one, total_two, total_router, total_table = (
        small[split[i] : split[i + 1]] for i in range(4)
    )
    grad_table = lax.dynamic_slice_in_dim(
        total_table.reshape(-1, bucket_count), tp_index * head_count, head_count, 0
    ).T
    return (
        result.astype(BF16),
        grad_inputs,
        total_one,
        total_two,
        attn_sum[0],
        attn_sum[1],
        attn_sum[2],
        attn_sum[3].T,
        grad_table,
        total_router.reshape(expert_count, model_width).T,
        inner_sum,
        jnp.transpose(outer_sum, (0, 2, 1)),
    )


USE_GRID = True

def solution(mesh):
    placed = (
        P(("fsdp", "tp"), None),
        P(("fsdp", "tp"), None),
        P(),
        P(),
        P("fsdp", "tp"),
        P("fsdp", "tp"),
        P("fsdp", "tp"),
        P("tp", "fsdp"),
        P(None, "tp"),
        P(),
        P(None, "fsdp", "tp"),
        P(None, "tp", "fsdp"),
        P("fsdp", None),
        P("fsdp"),
        P("fsdp"),
        P(),
    )
    return jax.shard_map(
        on_device,
        mesh=mesh,
        in_specs=placed,
        out_specs=(
            P(("fsdp", "tp"), None),
            P(("fsdp", "tp"), None),
            P(),
            P(),
            P("fsdp", "tp"),
            P("fsdp", "tp"),
            P("fsdp", "tp"),
            P("tp", "fsdp"),
            P(None, "tp"),
            P(),
            P(None, "fsdp", "tp"),
            P(None, "tp", "fsdp"),
        ),
        check_vma=False,
    )
```

```python
import functools
import math

import jax
import jax.numpy as jnp
from jax import lax
from jax.experimental import pallas as pl
from jax.experimental.pallas import tpu as pltpu
from jax.sharding import PartitionSpec as P

HD = 64
CAP = 192
EPSILON = 1e-06
MASKED = -1e30
HIGHEST = lax.Precision.HIGHEST
F32 = jnp.float32
BF16 = jnp.bfloat16
NT = (((1,), (1,)), ((), ()))
TN = (((0,), (0,)), ((), ()))


def rms_stats(values):
    inverse = lax.rsqrt(jnp.mean(values * values, axis=-1, keepdims=True) + EPSILON)
    return (values * inverse, inverse)


def rms_back(grad_hat, normed, inverse):
    return inverse * (grad_hat - normed * jnp.mean(grad_hat * normed, axis=-1, keepdims=True))


def tp_swap(values):
    return lax.ppermute(values, "tp", [(0, 1), (1, 0)])


def tp_gather(values):
    other = tp_swap(values)
    first = lax.axis_index("tp") == 0
    low = jnp.where(first, values, other)
    high = jnp.where(first, other, values)
    return jnp.concatenate([low, high], axis=0)


def tp_scatter(values):
    half = values.shape[0] // 2
    me = lax.axis_index("tp")
    away = lax.dynamic_slice_in_dim(values, (1 - me) * half, half, 0)
    keep = lax.dynamic_slice_in_dim(values, me * half, half, 0)
    return keep + tp_swap(away)


def grid_place():
    index = lax.axis_index("fsdp")
    return index // 4, (index // 2) % 2, index % 2


def flip(values, bit):
    return lax.ppermute(values, "fsdp", [(i, i ^ bit) for i in range(16)])


def z_shift(values, step):
    return lax.ppermute(values, "fsdp", [(i, (i + 4 * step) % 16) for i in range(16)])


def add_low(left, right):
    return (left.astype(F32) + right.astype(F32)).astype(BF16)


def fsdp_gather(shard):
    count = shard.shape[0] // 2
    if lax.axis_size("fsdp") != 16:
        full = lax.all_gather(shard, "fsdp", axis=1, tiled=True)
        return full[:count], full[count:]
    z_at, y_at, x_at = grid_place()
    one, two, three = (z_shift(shard, step) for step in (1, 2, 3))
    line = [three, two, one, shard, three, two, one]

    def column(part):
        stacked = jnp.stack([item[part] for item in line], axis=1)
        return lax.dynamic_slice_in_dim(stacked, 3 - z_at, 4, 1)

    def spread(part, place, axis, bit):
        other = flip(part, bit)
        low = jnp.where(place == 0, part, other)
        high = jnp.where(place == 0, other, part)
        return jnp.stack([low, high], axis=axis)

    first = spread(spread(column(slice(0, count)), x_at, 2, 1), y_at, 2, 2)
    second = spread(spread(column(slice(count, None)), y_at, 2, 2), x_at, 3, 1)
    return tuple(
        part.reshape(count, 16 * shard.shape[1], shard.shape[2]) for part in (first, second)
    )


def fold_parts(part, place, axis):
    away = lax.dynamic_index_in_dim(part, 1 - place, axis, False)
    keep = lax.dynamic_index_in_dim(part, place, axis, False)
    return away, keep


def scatter_first(halves):
    _, y_at, x_at = grid_place()
    first, second = (
        half.reshape((half.shape[0], 4, 2, 2, half.shape[1] // 16, half.shape[2]))
        for half in halves
    )
    return fold_parts(first, x_at, 3) + fold_parts(second, y_at, 2)


def scatter_second(parts):
    _, y_at, x_at = grid_place()
    away_one, keep_one, away_two, keep_two = parts
    first = add_low(keep_one, flip(away_one, 1))
    second = add_low(keep_two, flip(away_two, 2))
    return fold_parts(first, y_at, 2) + fold_parts(second, x_at, 2)


def scatter_third(parts):
    z_at, _, _ = grid_place()
    away_one, keep_one, away_two, keep_two = parts
    first = add_low(keep_one, flip(away_one, 2))
    second = add_low(keep_two, flip(away_two, 1))
    column = jnp.concatenate([first, second], axis=0)

    def pick(step):
        return lax.dynamic_index_in_dim(column, (z_at + step) % 4, 1, False)

    total = pick(0).astype(F32)
    for step in (1, 2, 3):
        total = total + z_shift(pick(step), step).astype(F32)
    return total


def plain_scatter(halves):
    full = jnp.concatenate(halves, axis=0)
    return lax.psum_scatter(full, "fsdp", scatter_dimension=1, tiled=True).astype(F32)


def after(values, earlier):
    return lax.optimization_barrier((values, earlier))


def sum_all(values):
    if lax.axis_size("fsdp") != 16:
        return lax.psum(values, ("fsdp", "tp"))
    values = values + tp_swap(values)
    for bit in (1, 2, 4, 8):
        values = values + flip(values, bit)
    return values


def head_weights(query, key, window, same, rows):
    scale = 1.0 / math.sqrt(HD)
    skew = pltpu.roll(
        jnp.broadcast_to(window, (rows, rows)), 0, 1, stride=1, stride_axis=0
    )
    scores = lax.dot_general(query, key, NT, preferred_element_type=F32) * scale + skew
    scores = jnp.where(same, scores, MASKED)
    raised = jnp.exp(scores - jnp.max(scores, axis=-1, keepdims=True))
    return raised / jnp.sum(raised, axis=-1, keepdims=True)


def attend_kernel(q_ref, k_ref, v_ref, win_ref, col_ref, row_ref, o_ref):
    rows = q_ref.shape[0]
    same = col_ref[...] == row_ref[...]
    mixed = []
    for head in range(2):
        part = slice(head * HD, (head + 1) * HD)
        weights = head_weights(
            q_ref[:, part], k_ref[:, part], win_ref[0, head : head + 1, :], same, rows
        )
        mixed.append(
            jnp.dot(weights.astype(BF16), v_ref[:, part], preferred_element_type=F32)
        )
    o_ref[...] = jnp.concatenate(mixed, axis=1).astype(BF16)


def attend_back_kernel(
    q_ref, k_ref, v_ref, do_ref, win_ref, col_ref, row_ref, dq_ref, dk_ref, dv_ref, sums_ref
):
    rows = q_ref.shape[0]
    scale = 1.0 / math.sqrt(HD)
    same = col_ref[...] == row_ref[...]
    all_dq, all_dk, all_dv, all_sums = [], [], [], []
    for head in range(2):
        part = slice(head * HD, (head + 1) * HD)
        query, key, value, grad = q_ref[:, part], k_ref[:, part], v_ref[:, part], do_ref[:, part]
        weights = head_weights(query, key, win_ref[0, head : head + 1, :], same, rows)
        low = weights.astype(BF16)
        grad_weights = lax.dot_general(grad, value, NT, preferred_element_type=F32)
        inner = jnp.sum(weights * grad_weights, axis=-1, keepdims=True)
        grad_scores = (weights * (grad_weights - inner)).astype(BF16)
        all_dq.append(jnp.dot(grad_scores, key, preferred_element_type=F32) * scale)
        all_dk.append(
            lax.dot_general(grad_scores, query, TN, preferred_element_type=F32) * scale
        )
        all_dv.append(lax.dot_general(low, grad, TN, preferred_element_type=F32))
        fold = grad_scores.astype(F32)
        count = rows
        while count > 8:
            count //= 2
            fold = fold[:count] + pltpu.roll(fold[count:], rows - count, 1)
        total = fold[0:1]
        for line in range(1, 8):
            total = total + pltpu.roll(fold, rows - line, 1)[line : line + 1]
        all_sums.append(total)
    dq_ref[...] = jnp.concatenate(all_dq, axis=1).astype(BF16)
    dk_ref[...] = jnp.concatenate(all_dk, axis=1).astype(BF16)
    dv_ref[...] = jnp.concatenate(all_dv, axis=1).astype(BF16)
    sums_ref[0] = jnp.concatenate(all_sums, axis=0)


def attend_call(kernel, wide_out, sums_out, wide_in, window, seg_col, seg_row):
    rows, width = wide_in[0].shape
    steps = width // (2 * HD)
    wide = pl.BlockSpec((rows, 2 * HD), lambda i: (0, i))
    lines = pl.BlockSpec((1, 2, rows), lambda i: (i, 0, 0))
    flops = 2 * 2 * rows * rows * width * (2 if wide_out == 1 else 5)
    return pl.pallas_call(
        kernel,
        grid=(steps,),
        in_specs=[wide] * len(wide_in)
        + [
            lines,
            pl.BlockSpec((rows, 1), lambda i: (0, 0)),
            pl.BlockSpec((1, rows), lambda i: (0, 0)),
        ],
        out_specs=[wide] * wide_out + [lines] * sums_out,
        out_shape=[jax.ShapeDtypeStruct((rows, width), BF16)] * wide_out
        + [jax.ShapeDtypeStruct((steps, 2, rows), F32)] * sums_out,
        cost_estimate=pl.CostEstimate(
            flops=flops, bytes_accessed=2 * rows * width * 8, transcendentals=rows * rows * 6
        ),
        compiler_params=pltpu.CompilerParams(vmem_limit_bytes=48 * 1024 * 1024),
    )(*wide_in, window, seg_col, seg_row)


def on_device(
    tokens,
    cotangent,
    gain_attn,
    gain_moe,
    w_query,
    w_key,
    w_value,
    w_output,
    bias_table,
    router,
    w_in,
    w_out,
    lengths,
    routes,
    slots,
    buckets,
):
    row_count, model_width = tokens.shape
    group_rows = routes.shape[0]
    bucket_count, head_count = bias_table.shape
    expert_count = router.shape[1]
    slot_count = expert_count * CAP
    n_fsdp = lax.axis_size("fsdp")
    span_len = buckets.shape[0]
    max_len = (span_len + 1) // 2
    tp_index = lax.axis_index("tp")
    positions = jnp.arange(group_rows, dtype=jnp.int32)
    expert_ids = jnp.arange(expert_count, dtype=jnp.int32)

    attn_shard = jnp.stack([w_query, w_key, w_value, w_output.T])
    attn_low, attn_high = fsdp_gather(attn_shard)
    inner_halves = fsdp_gather(w_in)
    outer_halves = fsdp_gather(jnp.transpose(w_out, (0, 2, 1)))
    attn_full = (attn_low[0], attn_low[1], attn_high[0], attn_high[1])
    on_grid = n_fsdp == 16
    half_count = expert_count // 2

    inputs = tokens.astype(F32)
    gain_one = gain_attn.astype(F32)
    gain_two = gain_moe.astype(F32)
    normed_one, inverse_one = rms_stats(inputs)
    scaled_one = (normed_one * gain_one).astype(BF16)
    rows_one = tp_gather(scaled_one)

    bounds = jnp.cumsum(lengths[0])
    segment = jnp.sum((positions[:, None] >= bounds[None, :]).astype(jnp.int32), axis=1)
    seg_col, seg_row = segment[:, None], segment[None, :]
    bucket_ids = jnp.arange(bucket_count, dtype=jnp.int32)
    window_buckets = jnp.concatenate(
        [
            buckets[max_len - 1 :],
            jnp.full((group_rows - span_len,), -1, jnp.int32),
            buckets[: max_len - 1],
        ]
    )
    window_hot = (window_buckets[:, None] == bucket_ids[None, :]).astype(F32)
    window = jnp.dot(window_hot, bias_table.astype(F32), precision=HIGHEST).T.reshape(
        head_count // 2, 2, group_rows
    )

    queries, keys_all, values_all = (
        jnp.dot(rows_one, attn_full[i], preferred_element_type=F32).astype(BF16) for i in range(3)
    )
    (mixed_out,) = attend_call(
        attend_kernel, 1, 0, (queries, keys_all, values_all), window, seg_col, seg_row
    )
    attn_part = lax.dot_general(mixed_out, attn_full[3], NT, preferred_element_type=F32)
    hidden = inputs + tp_scatter(attn_part)
    normed_two, inverse_two = rms_stats(hidden)
    scaled_two = (normed_two * gain_two).astype(BF16)
    rows_two = tp_gather(scaled_two)

    own_routes = lax.dynamic_slice_in_dim(routes, tp_index * row_count, row_count, 0)
    chances = jax.nn.softmax(jnp.dot(scaled_two, router, preferred_element_type=F32), axis=-1)
    own_hot = (own_routes[:, None] == expert_ids[None, :]).astype(F32)
    gate_val = jnp.sum(chances * own_hot, axis=-1, keepdims=True)

    kept_mask = slots >= 0
    places = jnp.where(kept_mask, routes * CAP + slots, -1)
    slot_ids = jnp.arange(slot_count, dtype=jnp.int32)
    dispatch = (slot_ids[:, None] == places[None, :]).astype(BF16)
    collect = (places[:, None] == slot_ids[None, :]).astype(BF16)

    def to_slots(rows):
        return (
            jnp.dot(dispatch, rows, preferred_element_type=F32)
            .astype(BF16)
            .reshape(expert_count, CAP, model_width)
        )

    def to_tokens(rows):
        high = rows.astype(BF16)
        low = (rows - high.astype(F32)).astype(BF16)
        return jnp.dot(collect, high, preferred_element_type=F32) + jnp.dot(
            collect, low, preferred_element_type=F32
        )

    def halves_of(values):
        return values[:half_count], values[half_count:]

    def rows_of(parts):
        return jnp.concatenate(parts, axis=0).reshape(slot_count, model_width)

    def product(spec, left, right):
        return jnp.einsum(spec, left, right, preferred_element_type=F32)

    buffers = halves_of(to_slots(rows_two))
    pre_acts = [product("ecd,edf->ecf", b, w) for b, w in zip(buffers, inner_halves)]
    activated = [jax.nn.gelu(pre).astype(BF16) for pre in pre_acts]
    expert_rows = rows_of(
        [product("ecf,edf->ecd", a, w) for a, w in zip(activated, outer_halves)]
    )
    expert_val = tp_scatter(to_tokens(expert_rows))
    result = hidden + gate_val * expert_val

    grad_out = cotangent.astype(F32)
    grad_gate = jnp.sum(grad_out * expert_val, axis=-1, keepdims=True)
    grad_expert = (gate_val * grad_out).astype(BF16)
    grad_slots = halves_of(to_slots(tp_gather(grad_expert)))
    outer_grads = [
        product("ecd,ecf->edf", g, a).astype(BF16) for g, a in zip(grad_slots, activated)
    ]
    grad_acts = [product("ecd,edf->ecf", g, w) for g, w in zip(grad_slots, outer_halves)]
    grad_pres = [
        jax.vjp(jax.nn.gelu, pre)[1](grad)[0].astype(BF16)
        for pre, grad in zip(pre_acts, grad_acts)
    ]
    inner_grads = [
        product("ecd,ecf->edf", b, g).astype(BF16) for b, g in zip(buffers, grad_pres)
    ]
    grad_buffer = rows_of(
        [product("ecf,edf->ecd", g, w) for g, w in zip(grad_pres, inner_halves)]
    )
    grad_logits = (grad_gate * gate_val * (own_hot - chances)).astype(BF16)
    grad_router = jnp.einsum("td,te->de", scaled_two, grad_logits, preferred_element_type=F32)
    grad_scaled_two = tp_scatter(to_tokens(grad_buffer)) + jnp.einsum(
        "te,de->td", grad_logits, router, preferred_element_type=F32
    )
    grad_gain_two = jnp.sum(grad_scaled_two * normed_two, axis=0)
    grad_hidden = grad_out + rms_back(grad_scaled_two * gain_two, normed_two, inverse_two)
    grad_attn = tp_gather(grad_hidden.astype(BF16))
    grad_mixed = jnp.dot(grad_attn, attn_full[3], preferred_element_type=F32).astype(BF16)
    if on_grid:
        outer_parts = scatter_second(scatter_first(outer_grads))
        (inner_grads, grad_mixed), outer_parts = after((inner_grads, grad_mixed), outer_parts)
        outer_sum = scatter_third(outer_parts)
        inner_parts = scatter_second(scatter_first(inner_grads))
    grad_queries, grad_keys, grad_values, window_sums = attend_call(
        attend_back_kernel,
        3,
        1,
        (queries, keys_all, values_all, grad_mixed),
        window,
        seg_col,
        seg_row,
    )
    attn_grads = [
        jnp.stack(
            [lax.dot_general(left, right, TN, preferred_element_type=F32) for left, right in pairs]
        ).astype(BF16)
        for pairs in (
            ((rows_one, grad_queries), (rows_one, grad_keys)),
            ((rows_one, grad_values), (grad_attn, mixed_out)),
        )
    ]
    if on_grid:
        attn_grads, inner_parts = after(attn_grads, inner_parts)
        inner_sum = scatter_third(inner_parts)
        attn_sum = scatter_third(scatter_second(scatter_first(attn_grads)))
    else:
        outer_sum, inner_sum, attn_sum = (
            plain_scatter(grads) for grads in (outer_grads, inner_grads, attn_grads)
        )
    grad_one_part = sum(
        lax.dot_general(grads, attn_full[i], NT, preferred_element_type=F32)
        for i, grads in enumerate((grad_queries, grad_keys, grad_values))
    )
    grad_scaled_one = tp_scatter(grad_one_part)
    grad_gain_one = jnp.sum(grad_scaled_one * normed_one, axis=0)
    grad_inputs = grad_hidden + rms_back(grad_scaled_one * gain_one, normed_one, inverse_one)

    grad_table_here = jnp.dot(
        window_sums.reshape(head_count, group_rows), window_hot, precision=HIGHEST
    )
    table_full = lax.dynamic_update_slice_in_dim(
        jnp.zeros((head_count * lax.axis_size("tp"), bucket_count), F32),
        grad_table_here,
        tp_index * head_count,
        0,
    )
    pieces = [grad_gain_one, grad_gain_two, grad_router.T.reshape(-1), table_full.reshape(-1)]
    small = sum_all(jnp.concatenate(pieces))
    split = [0]
    for piece in pieces:
        split.append(split[-1] + piece.shape[0])
    total_one, total_two, total_router, total_table = (
        small[split[i] : split[i + 1]] for i in range(4)
    )
    grad_table = lax.dynamic_slice_in_dim(
        total_table.reshape(-1, bucket_count), tp_index * head_count, head_count, 0
    ).T
    return (
        result.astype(BF16),
        grad_inputs,
        total_one,
        total_two,
        attn_sum[0],
        attn_sum[1],
        attn_sum[2],
        attn_sum[3].T,
        grad_table,
        total_router.reshape(expert_count, model_width).T,
        inner_sum,
        jnp.transpose(outer_sum, (0, 2, 1)),
    )


def solution(mesh):
    placed = (
        P(("fsdp", "tp"), None),
        P(("fsdp", "tp"), None),
        P(),
        P(),
        P("fsdp", "tp"),
        P("fsdp", "tp"),
        P("fsdp", "tp"),
        P("tp", "fsdp"),
        P(None, "tp"),
        P(),
        P(None, "fsdp", "tp"),
        P(None, "tp", "fsdp"),
        P("fsdp", None),
        P("fsdp"),
        P("fsdp"),
        P(),
    )
    return jax.shard_map(
        on_device,
        mesh=mesh,
        in_specs=placed,
        out_specs=(
            P(("fsdp", "tp"), None),
            P(("fsdp", "tp"), None),
            P(),
            P(),
            P("fsdp", "tp"),
            P("fsdp", "tp"),
            P("fsdp", "tp"),
            P("tp", "fsdp"),
            P(None, "tp"),
            P(),
            P(None, "fsdp", "tp"),
            P(None, "tp", "fsdp"),
        ),
        check_vma=False,
    )
```
